512 devices in a mesh: tm: 64 (over y, z), space: 8 (over x, core).
Axes of the slice: x: 4, y: 8, z: 8, core: 2. Of those that a mesh axis runs over, the one named last changes fastest.
Arguments:
- fields: bfloat16 [16384, 3, 12288], P('tm', None, 'space'), may hold values from -100 to 100
- test_matrix: bfloat16 [64, 3, 12288], P(None, None, 'space'), may hold values from -0.03125 to 0.03125
Outputs:
- pcs: float32 [64, 16384], P(None, 'tm')
- energy: float32 [3, 12288], P(None, 'space')
The draws below stay inside these ranges and needn't reach their ends.
All inputs are finite; a program needn't handle non-finite values.
Results may differ from the reference program's by a relative error of at most 0.0035.
Values may be sent and summed in bfloat16 or wider, within the bound.
A program may use at most 64 MiB of HBM per device.

```python
import math
import jax
import jax.numpy as jnp
import numpy as np
from jax import lax

FIELDS = 3
K = 64
HALF = 100
ITERS = 2
TIMES = 16384
G = 12288


def draw_fields(key, part):
    key = jax.random.fold_in(key, 11)
    noise_key, column_key = jax.random.split(key, 2)
    moments = jnp.arange(TIMES, dtype=jnp.float32) / max(TIMES - 1, 1)
    time_scale = jnp.exp(jnp.log(3.0) * moments)[:, None, None]
    column_scale = jnp.exp(jax.random.uniform(column_key, (FIELDS, G), dtype=jnp.float32) * jnp.log(10.0))
    noise = jax.random.normal(noise_key, (TIMES, FIELDS, G), dtype=jnp.float32)
    values = jnp.clip(0.8 * time_scale * column_scale[None, :, :] * noise, -100.0, 100.0)
    return values.astype(jnp.bfloat16)


def block_levels(stream_key, shape, shards, least, high):
    factor_of = 1.0
    for axis_at, blocks in shards:
        heights = jax.random.uniform(jax.random.fold_in(jax.random.fold_in(stream_key, 6), axis_at), (blocks,), jnp.float32, least / len(shards), high / len(shards))
        factor_of = factor_of * jnp.repeat(jnp.exp(heights), shape[axis_at] // blocks).reshape((-1,) + (1,) * (len(shape) - 1 - axis_at))
    return factor_of


def gaussian(own_key, extent, scale, bound, cuts=(), held_as=jnp.bfloat16):
    values = scale * jax.random.normal(own_key, extent, jnp.float32)
    if cuts:
        values = values * block_levels(own_key, extent, cuts, -0.22, 0.18)
    return jnp.clip(values, -bound, bound).astype(held_as)


def setup_inputs(seed: int = 0) -> dict:
    streams_of = jax.random.split(jax.random.key(seed), 3)
    fields = draw_fields(jax.random.fold_in(streams_of[2], 71), 0)
    test_matrix = gaussian(streams_of[1], (K, FIELDS, G), (FIELDS * G) ** -0.5, 0.03125, ((2, 8),))
    return {"fields": fields, "test_matrix": test_matrix}


low_cutoff = 1.0 / 96.0
high_cutoff = 1.0 / 24.0

def lanczos_band(row_count, half_width):
    lag_table = (np.arange(row_count + 2 * half_width)[None, :] - np.arange(row_count)[:, None] - half_width) * 1.0
    safe_lag = np.where(lag_table == 0, 1.0, lag_table)
    response = (np.sin(2 * np.pi * high_cutoff * safe_lag) - np.sin(2 * np.pi * low_cutoff * safe_lag)) / (np.pi * safe_lag)
    response = np.where(lag_table == 0, 2.0 * (high_cutoff - low_cutoff), response)
    ratio = np.pi * safe_lag / (half_width + 1)
    sigma_factor = np.where(lag_table == 0, 1.0, np.sin(ratio) / ratio)
    return np.where(np.abs(lag_table) <= half_width, response * sigma_factor, 0.0).astype(np.float32)

def orthonormal(sketch):
    gram_total = jnp.dot(sketch, sketch.T, precision=lax.Precision.HIGHEST)
    lower_factor = jnp.linalg.cholesky(gram_total)
    return jax.scipy.linalg.solve_triangular(lower_factor, sketch, lower=True)

def reference(fields, test_matrix):
    time_total = fields.shape[0]
    flat_width = FIELDS * G
    flat_fields = fields.reshape(time_total, flat_width)
    padded = jnp.pad(flat_fields, ((HALF, HALF), (0, 0)))
    block_rows = math.gcd(time_total, 512)
    filter_band = jnp.asarray(lanczos_band(block_rows, HALF)).astype(jnp.bfloat16)

    def filter_block(block_index):
        window = lax.dynamic_slice_in_dim(padded, (block_index * block_rows).astype(jnp.int32), block_rows + 2 * HALF, 0)
        return jnp.dot(filter_band.astype(jnp.float32), window.astype(jnp.float32), preferred_element_type=jnp.float32).astype(jnp.bfloat16)
    filtered = lax.map(filter_block, jnp.arange(time_total // block_rows, dtype=jnp.int32)).reshape(time_total, flat_width)
    contract = (((1,), (1,)), ((), ()))
    flat_test = test_matrix.reshape(K, flat_width)
    sketch = lax.dot_general(flat_test.astype(jnp.float32), filtered.astype(jnp.float32), contract, preferred_element_type=jnp.float32)
    orth_basis = orthonormal(sketch)
    for iteration in range(ITERS):
        loadings = jnp.dot(orth_basis.astype(jnp.bfloat16).astype(jnp.float32), filtered.astype(jnp.float32), preferred_element_type=jnp.float32)
        sketch = lax.dot_general(loadings.astype(jnp.bfloat16).astype(jnp.float32), filtered.astype(jnp.float32), contract, preferred_element_type=jnp.float32)
        orth_basis = orthonormal(sketch)
    final = jnp.dot(orth_basis.astype(jnp.bfloat16).astype(jnp.float32), filtered.astype(jnp.float32), preferred_element_type=jnp.float32)
    energy = (lax.optimization_barrier(jnp.sum(final * final, axis=0)) / time_total).reshape(FIELDS, G)
    pcs = orth_basis * math.sqrt(time_total)
    return (pcs, energy)
```

```python
import functools
import math

import jax
import jax.numpy as jnp
import numpy as np
from jax import lax
from jax.experimental import pallas as pl
from jax.experimental.pallas import tpu as pltpu
from jax.sharding import PartitionSpec as P

MESH = pl.DeviceIdType.MESH
HALF = 100
ITERS = 2
PAD = 128
low_cutoff = 1.0 / 96.0
high_cutoff = 1.0 / 24.0

SIDE = 8
PARTS = 8
K = 64
ROWS = 256
WIDE = 4608
PACK = WIDE // 2
HALFROWS = PACK // 2
CHUNK = HALFROWS // SIDE
MAIN = 16
LEFT = MAIN * SIDE
F32, BF16 = jnp.float32, jnp.bfloat16
HI = lax.Precision.HIGHEST
NT = (((1,), (1,)), ((), ()))
TN = (((0,), (0,)), ((), ()))
ORDER = (4, 3, 5, 2, 6, 1, 7)


def lanczos(half_width):
    lag = np.arange(-half_width, half_width + 1) * 1.0
    safe = np.where(lag == 0, 1.0, lag)
    response = (np.sin(2 * np.pi * high_cutoff * safe) - np.sin(2 * np.pi * low_cutoff * safe)) / (np.pi * safe)
    response = np.where(lag == 0, 2.0 * (high_cutoff - low_cutoff), response)
    ratio = np.pi * safe / (half_width + 1)
    sigma = np.where(lag == 0, 1.0, np.sin(ratio) / ratio)
    return (response * sigma).astype(np.float32)


def band_matrix():
    lag = np.arange(3 * ROWS)[:, None] - np.arange(ROWS + 2 * PAD)[None, :] - (ROWS - PAD)
    taps = lanczos(HALF)[np.clip(lag + HALF, 0, 2 * HALF)]
    return np.where(np.abs(lag) <= HALF, taps, 0.0).astype(np.float32)


def split3(x):
    hi = x.astype(BF16)
    rest = x - hi.astype(F32)
    mid = rest.astype(BF16)
    low = (rest - mid.astype(F32)).astype(BF16)
    return jnp.concatenate([hi, mid, low], axis=0)


def filter_rows(x, band):
    out = jnp.dot(split3(x), band, preferred_element_type=F32)
    return out[0:K] + out[K : 2 * K] + out[2 * K : 3 * K]


def factor(gram):
    row_id = lax.broadcasted_iota(jnp.int32, (K, 2 * K), 0)
    lane_id = lax.broadcasted_iota(jnp.int32, (K, 2 * K), 1)
    a = jnp.where(lane_id < K, gram, 0.0) + jnp.where(lane_id == row_id + K, 1.0, 0.0)
    blocks = [a[8 * b : 8 * b + 8] for b in range(K // 8)]
    sub_id = lax.broadcasted_iota(jnp.int32, (8, 2 * K), 0)
    for j in range(K):
        b, r = divmod(j, 8)
        inv = lax.rsqrt(blocks[b][r : r + 1, j : j + 1])
        row = blocks[b][r : r + 1, :] * inv
        scaled = row * inv
        for c in range(b, K // 8):
            col = blocks[c][:, j : j + 1]
            nxt = blocks[c] - col * scaled
            if c == b:
                nxt = jnp.where(sub_id > r, nxt, jnp.where(sub_id == r, row, blocks[c]))
            blocks[c] = nxt
    return jnp.concatenate(blocks, axis=0)


def kernel(
    x_hbm, t_hbm, band_ref, pcs_ref, eb,
    xv, tv, xt, lbt, rbuf, srr, rext, s2, wt, gzs, gzr, gys, gyr, gfull, v1, r1, v2, r2, res, linv2, racc,
    in_sem,
    sr_s, sr_r, ah_s, ah_r, gz_s, gz_r, gy_s, gy_r, gs_s, gs_r,
    p1_s, p1_r, p2_s, p2_r, a1_s, a1_r, a2_s, a2_r, e1_s, e1_r, e2_s, e2_r,
):
    t, s = lax.axis_index("tm"), lax.axis_index("space")
    y, z = t // SIDE, t % SIDE
    times = SIDE * SIDE

    def at_z(p):
        return (y * SIDE + p, s)

    def at_y(p):
        return (p * SIDE + z, s)

    first = ((z, at_z), (y, at_y))
    second = ((y, at_y), (z, at_z))
    t_next, t_prev = (t + 1) % times, (t + times - 1) % times

    loads = []
    for f in range(3):
        cols = pl.ds(f * (WIDE // 3), WIDE // 3)
        loads.append(pltpu.make_async_copy(x_hbm.at[f], xv.at[:, cols], in_sem.at[f]))
        loads.append(pltpu.make_async_copy(t_hbm.at[f], tv.at[:, cols], in_sem.at[3 + f]))
    for c in loads:
        c.start()

    barrier = pltpu.get_barrier_semaphore()
    greet = []
    for d in range(1, SIDE):
        greet += [at_z((z + d) % SIDE), at_y((y + d) % SIDE), (t, (s + d) % PARTS)]
    for d in range(PARTS):
        greet += [(t_next, (s + d) % PARTS), (t_prev, (s + d) % PARTS)]
    for dev in greet:
        pl.semaphore_signal(barrier, inc=1, device_id=dev, device_id_type=MESH)

    s2[pl.ds(K, K), :] = jnp.zeros((K, ROWS), F32)
    wt[...] = jnp.zeros((4 * K, 2 * ROWS), BF16)
    for c in loads:
        c.wait()
    rbuf[...] = lax.dot_general(tv[...], xv[...], NT, preferred_element_type=F32)
    pl.semaphore_wait(barrier, len(greet))

    def copy(src, dst, send, recv, dev):
        return pltpu.make_async_remote_copy(
            src_ref=src, dst_ref=dst, send_sem=send, recv_sem=recv, device_id=dev, device_id_type=MESH
        )

    my_rows = pl.ds(pl.multiple_of(s * 8, 8), 8)

    def iteration(i, carry):
        sends = []
        for d in range(1, PARTS):
            p = (s + d) % PARTS
            c = copy(rbuf.at[pl.ds(pl.multiple_of(p * 8, 8), 8)], srr.at[d - 1], sr_s.at[d - 1], sr_r.at[d - 1], (t, p))
            c.start()
            sends.append(c)

        @pl.when(i == 0)
        def _():
            for j in range(PACK // 128):
                for side in range(2):
                    xt[pl.ds(j * 128, 128), pl.ds(side * ROWS, ROWS)] = xv[:, pl.ds(side * PACK + j * 128, 128)].T

        total = rbuf[my_rows, :]
        for d in range(1, PARTS):
            sends[d - 1].wait_recv()
            total = total + srr[d - 1]
        rext[my_rows, pl.ds(ROWS, ROWS)] = total

        gath = []
        mine = rext.at[my_rows, pl.ds(ROWS, ROWS)]
        n = 0
        for d in range(PARTS):
            p = (s + d) % PARTS
            for tt, lane in ((t_next, 0), (t_prev, 2 * ROWS), (t, ROWS)):
                if d == 0 and lane == ROWS:
                    continue
                c = copy(mine, rext.at[my_rows, pl.ds(lane, ROWS)], ah_s.at[n], ah_r.at[n], (tt, p))
                c.start()
                gath.append(c)
                n += 1
        for c in gath:
            c.wait_recv()
        for c in sends + gath:
            c.wait_send()

        hour = lax.broadcasted_iota(jnp.int32, (1, ROWS + 2 * PAD), 1) + (t * ROWS - PAD)
        inside = jnp.logical_and(hour >= 0, hour < times * ROWS)
        r_in = rext[...]
        slab = lax.broadcasted_iota(jnp.int32, (1, 3 * ROWS), 1) + (t - 1) * ROWS
        r_in = jnp.where(jnp.logical_and(slab >= 0, slab < times * ROWS), r_in, 0.0)
        s_ext = filter_rows(r_in, band_ref[...])
        s_ext = jnp.where(inside, s_ext, 0.0)
        s2[pl.ds(0, K), :] = s_ext[:, PAD : PAD + ROWS]
        gzs[...] = lax.dot_general(s2[my_rows, :], s2[...], NT, precision=HI, preferred_element_type=F32)
        gz = []
        for d in range(1, SIDE):
            c = copy(gzs, gzr.at[d - 1], gz_s.at[d - 1], gz_r.at[d - 1], at_z((z + d) % SIDE))
            c.start()
            gz.append(c)
        u = filter_rows(s_ext, band_ref[pl.ds(0, ROWS + 2 * PAD), pl.ds(0, ROWS)])
        u_hi = u.astype(BF16)
        u_mid = (u - u_hi.astype(F32)).astype(BF16)
        wt[pl.ds(0, K), pl.ds(0, ROWS)] = u_hi
        wt[pl.ds(K, K), pl.ds(ROWS, ROWS)] = u_hi
        wt[pl.ds(2 * K, K), pl.ds(0, ROWS)] = u_mid
        wt[pl.ds(3 * K, K), pl.ds(ROWS, ROWS)] = u_mid

        def product(h, p):
            rows = pl.ds(pl.multiple_of(h * HALFROWS + p * CHUNK, 16), CHUNK)
            out = lax.dot_general(xt[rows, :], wt[...], NT, preferred_element_type=F32)
            return out[:, 0:128] + out[:, 128:256]

        one = []
        for d in ORDER:
            for h in range(2):
                pos, dev = first[h]
                p = (pos + d) % SIDE
                v1[h, d] = product(h, p)
                c = copy(v1.at[h, d], r1.at[h, d - 1], p1_s.at[h, d - 1], p1_r.at[h, d - 1], dev(p))
                c.start()
                one.append((c, h, d))
        for h in range(2):
            v1[h, 0] = product(h, first[h][0])

        total = gzs[...]
        for d in range(1, SIDE):
            gz[d - 1].wait_recv()
            total = total + gzr[d - 1]
        gys[...] = total
        gy = []
        for d in range(1, SIDE):
            c = copy(gys, gyr.at[d - 1], gy_s.at[d - 1], gy_r.at[d - 1], at_y((y + d) % SIDE))
            c.start()
            gy.append(c)
        total = gys[...]
        for d in range(1, SIDE):
            gy[d - 1].wait_recv()
            total = total + gyr[d - 1]
        gfull[my_rows, :] = total
        gs = []
        for d in range(1, PARTS):
            c = copy(gfull.at[my_rows], gfull.at[my_rows], gs_s.at[d - 1], gs_r.at[d - 1], (t, (s + d) % PARTS))
            c.start()
            gs.append(c)

        for c, h, d in one:
            c.wait_recv()
        two = []
        for h in range(2):
            total = v1[h, 0]
            for d in range(1, SIDE):
                total = total + r1[h, d - 1]
            for q in range(SIDE):
                v2[h, q, pl.ds(0, MAIN)] = total[q * MAIN : (q + 1) * MAIN]
                v2[h, q, pl.ds(MAIN, MAIN)] = total[LEFT:CHUNK]
            pos, dev = second[h]
            for d in range(1, SIDE):
                q = (pos + d) % SIDE
                c = copy(v2.at[h, q], r2.at[h, d - 1], p2_s.at[h, d - 1], p2_r.at[h, d - 1], dev(q))
                c.start()
                two.append(c)

        for c in gs:
            c.wait_recv()
        aug = factor(gfull[...])
        lane_id = lax.broadcasted_iota(jnp.int32, (K, 2 * K), 1)
        low = jnp.where(lane_id >= K, aug, 0.0)
        linv2[pl.ds(0, K), :] = pltpu.roll(low, K, 1)
        linv2[pl.ds(K, K), :] = low

        for c in two:
            c.wait_recv()
        for h in range(2):
            total = v2[h, second[h][0]]
            for d in range(1, SIDE):
                total = total + r2[h, d - 1]
            res[pl.ds(2 * MAIN * h, 2 * MAIN), :] = total
        res[...] = lax.dot_general(res[...], linv2[...], NT, precision=HI, preferred_element_type=F32)
        for c in gz + gy + gs + two:
            c.wait_send()
        for c, h, d in one:
            c.wait_send()

        @pl.when(i < ITERS)
        def _():
            gat = []
            for h in range(2):
                base = h * HALFROWS + first[h][0] * CHUNK
                pos, dev = second[h]
                own = pl.ds(pl.multiple_of(base + pos * MAIN, MAIN), MAIN)
                lbt[own, :] = res[pl.ds(2 * MAIN * h, MAIN), :].astype(BF16)
                lbt[pl.ds(pl.multiple_of(base + LEFT, MAIN), MAIN), :] = res[pl.ds(2 * MAIN * h + MAIN, MAIN), :].astype(BF16)
                for d in ORDER:
                    c = copy(lbt.at[own], lbt.at[own], a1_s.at[h, d - 1], a1_r.at[h, d - 1], dev((pos + d) % SIDE))
                    c.start()
                    gat.append((c, h))
            out = []
            for h in range(2):
                for c, hh in gat:
                    if hh == h:
                        c.wait_recv()
                pos, dev = first[h]
                own = pl.ds(pl.multiple_of(h * HALFROWS + pos * CHUNK, 16), CHUNK)
                for d in ORDER:
                    c = copy(lbt.at[own], lbt.at[own], a2_s.at[h, d - 1], a2_r.at[h, d - 1], dev((pos + d) % SIDE))
                    c.start()
                    out.append(c)
            for c in out:
                c.wait_recv()
            prod = lax.dot_general(lbt[...], xt[...], TN, preferred_element_type=F32)
            rbuf[...] = prod[0:K, 0:ROWS] + prod[K : 2 * K, ROWS : 2 * ROWS]
            for c, h in gat:
                c.wait_send()
            for c in out:
                c.wait_send()

        return carry

    lax.fori_loop(0, ITERS + 1, iteration, 0)

    pcs_ref[...] = jnp.dot(linv2[pl.ds(0, K), :], s2[...], precision=HI, preferred_element_type=F32)
    square = res[...] * res[...]
    lane_id = lax.broadcasted_iota(jnp.int32, (K, 2 * K), 1)
    stack = jnp.concatenate([jnp.where(lane_id < K, square, 0.0), jnp.where(lane_id >= K, square, 0.0)], axis=0)
    sums = lax.dot_general(jnp.ones((8, 2 * K), F32), stack, NT, precision=HI, preferred_element_type=F32)
    own = z * SIDE + y
    eb[own] = sums[0:1, :]
    e1 = []
    for d in range(1, SIDE):
        c = copy(eb.at[own], eb.at[own], e1_s.at[d - 1], e1_r.at[d - 1], at_y((y + d) % SIDE))
        c.start()
        e1.append(c)
    for c in e1:
        c.wait_recv()
    e2 = []
    group = pl.ds(z * SIDE, SIDE)
    for d in range(1, SIDE):
        c = copy(eb.at[group], eb.at[group], e2_s.at[d - 1], e2_r.at[d - 1], at_z((z + d) % SIDE))
        c.start()
        e2.append(c)
    for c in e2:
        c.wait_recv()
    for c in e1 + e2:
        c.wait_send()


def body(fields, test_matrix):
    x = jnp.transpose(fields, (1, 0, 2))
    tm = jnp.transpose(test_matrix, (1, 0, 2))
    band = jnp.asarray(band_matrix()).astype(BF16)
    vm = pltpu.VMEM
    dma = pltpu.SemaphoreType.DMA
    seven, halves = (SIDE - 1,), (2, SIDE - 1)
    scratch = [
        vm((ROWS, WIDE), BF16), vm((K, WIDE), BF16), vm((PACK, 2 * ROWS), BF16), vm((PACK, 2 * K), BF16),
        vm((K, ROWS), F32), vm((PARTS - 1, 8, ROWS), F32), vm((K, 3 * ROWS), F32), vm((2 * K, ROWS), F32),
        vm((4 * K, 2 * ROWS), BF16),
        vm((8, 2 * K), F32), vm((SIDE - 1, 8, 2 * K), F32), vm((8, 2 * K), F32), vm((SIDE - 1, 8, 2 * K), F32), vm((K, 2 * K), F32),
        vm((2, SIDE, CHUNK, 128), F32), vm((2, SIDE - 1, CHUNK, 128), F32),
        vm((2, SIDE, 2 * MAIN, 128), F32), vm((2, SIDE - 1, 2 * MAIN, 128), F32),
        vm((K, 128), F32), vm((2 * K, 2 * K), F32), vm((8, 128), F32),
        dma((6,)),
        dma(seven), dma(seven), dma((3 * PARTS - 1,)), dma((3 * PARTS - 1,)),
        dma(seven), dma(seven), dma(seven), dma(seven), dma(seven), dma(seven),
        dma(halves), dma(halves), dma(halves), dma(halves), dma(halves), dma(halves), dma(halves), dma(halves),
        dma(seven), dma(seven), dma(seven), dma(seven),
    ]
    basis, parts = pl.pallas_call(
        kernel,
        out_shape=(
            jax.ShapeDtypeStruct((K, ROWS), F32),
            jax.ShapeDtypeStruct((SIDE * SIDE, 1, 128), F32),
        ),
        in_specs=[
            pl.BlockSpec(memory_space=pl.ANY),
            pl.BlockSpec(memory_space=pl.ANY),
            pl.BlockSpec(memory_space=pltpu.VMEM),
        ],
        out_specs=(pl.BlockSpec(memory_space=pltpu.VMEM), pl.BlockSpec(memory_space=pltpu.VMEM)),
        scratch_shapes=scratch,
        compiler_params=pltpu.CompilerParams(collective_id=0, has_side_effects=True, vmem_limit_bytes=48 << 20),
    )(x, tm, band)
    total_times = SIDE * SIDE * ROWS
    pcs = basis * math.sqrt(total_times)
    e = parts.reshape(SIDE, SIDE, 2, 2, 2, MAIN)
    main0 = jnp.transpose(e[:, :, :, 0, 0], (2, 0, 1, 3)).reshape(2, SIDE, LEFT)
    last0 = jnp.transpose(e[:, 0, :, 0, 1], (1, 0, 2))
    main1 = jnp.transpose(e[:, :, :, 1, 0], (2, 1, 0, 3)).reshape(2, SIDE, LEFT)
    last1 = jnp.transpose(e[0, :, :, 1, 1], (1, 0, 2))
    half0 = jnp.concatenate([main0, last0], axis=2).reshape(2, HALFROWS)
    half1 = jnp.concatenate([main1, last1], axis=2).reshape(2, HALFROWS)
    energy = jnp.concatenate([half0, half1], axis=1).reshape(3, WIDE // 3) / total_times
    return (pcs, energy)


def solution(mesh):
    return jax.shard_map(
        body,
        mesh=mesh,
        in_specs=(P("tm", None, "space"), P(None, None, "space")),
        out_specs=(P(None, "tm"), P(None, "space")),
        check_vma=False,
    )
```
